32 devices in a mesh: row: 8 (over z, x), col: 4 (over y, core).
Axes of the slice: x: 2, y: 2, z: 4, core: 2. Of those that a mesh axis runs over, the one named last changes fastest.
Arguments:
- gate_pre: bfloat16 [1024, 26624], P('col', 'row'), may hold values from -6 to 6
- up_pre: bfloat16 [1024, 26624], P('col', 'row'), may hold values from -6 to 6
- out_grad: bfloat16 [1024, 8192], P('row', 'col'), may hold values from -0.29882812 to 0.29882812
- w_gate: bfloat16 [8192, 26624], P('col', 'row'), may hold values from -0.0625 to 0.0625
- w_up: bfloat16 [8192, 26624], P('col', 'row'), may hold values from -0.0625 to 0.0625
- w_down: bfloat16 [26624, 8192], P('row', 'col'), may hold values from -1.5 to 1.5
Outputs:
- input_grad: bfloat16 [1024, 8192], P('row', 'col')
- down_wgrad: bfloat16 [26624, 8192], P('row', 'col')
The draws below stay inside these ranges and needn't reach their ends.
All inputs are finite; a program needn't handle non-finite values.
Results may differ from the reference program's by a relative error of at most 0.012.
Values may be sent and summed in bfloat16 or wider, within the bound.
A program may use at most 192 MiB of HBM per device.

```python
import jax
import jax.numpy as jnp

D = 8192
FF = 26624
TOKENS = 1024


def raised(drawn, rng, source, target, blocks, factor):
    owner, partner = [(jnp.arange(drawn.shape[axis_at]) // (drawn.shape[axis_at] // blocks)).reshape([-1 if axis == axis_at else 1 for axis in range(drawn.ndim)]) for axis_at in (source, target)]
    chosen = jax.random.permutation(rng, blocks)[partner]
    strong = (owner == chosen) | (owner == (partner + blocks // 2) % blocks)
    return jnp.where(strong, factor * drawn, drawn)


def level_of(key, shape, split, low, largest):
    gain, own = 1.0, jax.random.fold_in(key, 6)
    for dim, parts in split:
        heights = jnp.exp(jax.random.uniform(jax.random.fold_in(own, dim), (parts,), jnp.float32, low / len(split), largest / len(split)))
        gain = gain * jnp.repeat(heights, shape[dim] // parts).reshape([-1 if axis == dim else 1 for axis in range(len(shape))])
    return gain


def bell_draw(key, dims, deviation, limit, split=(), dtype=jnp.bfloat16):
    factor_of = level_of(key, dims, split, -0.22, 0.18) if split else 1.0
    result = jax.random.normal(key, dims, jnp.float32) * deviation * factor_of
    return jnp.minimum(jnp.maximum(result, -limit), limit).astype(dtype)


def noise_with(key, dims, scale, most, shards, heavy, dtype=jnp.bfloat16):
    result = scale * jax.random.normal(key, dims, jnp.float32)
    if shards:
        result = result * level_of(key, dims, shards, -0.22, 0.18)
    return jnp.clip(raised(result, jax.random.fold_in(key, 3), *heavy), -most, most).astype(dtype)


def setup_inputs(seed: int = 0) -> dict:
    arg_keys = jax.random.split(jax.random.key(seed), 7)
    return {
        "gate_pre": bell_draw(arg_keys[0], (TOKENS, FF), 1.0, 6.0, ((0, 4), (1, 8))),
        "up_pre": bell_draw(arg_keys[1], (TOKENS, FF), 1.0, 6.0, ((0, 4), (1, 8))),
        "out_grad": noise_with(arg_keys[2], (TOKENS, D), 0.04, 0.29882812, ((0, 8), (1, 4)), (1, 0, 8, 2.0)),
        "w_gate": bell_draw(arg_keys[3], (D, FF), D ** -0.5, 0.0625, ((0, 4), (1, 8))),
        "w_up": bell_draw(arg_keys[4], (D, FF), D ** -0.5, 0.0625, ((0, 4), (1, 8))),
        "w_down": bell_draw(arg_keys[5], (FF, D), (max(D // 512, 1)) ** -0.5, 1.5, ((0, 8), (1, 4))),
    }


def reference(gate_pre, up_pre, out_grad, w_gate, w_up, w_down):
    hidden_grad = jnp.dot(out_grad, w_down.T, preferred_element_type=jnp.float32).astype(jnp.bfloat16)
    gate_f = gate_pre.astype(jnp.float32)
    up_f = up_pre.astype(jnp.float32)
    sig = jax.nn.sigmoid(gate_f)
    grad_f = hidden_grad.astype(jnp.float32)
    gate_grad = (grad_f * up_f * sig * (1.0 + gate_f * (1.0 - sig))).astype(jnp.bfloat16)
    up_grad = (grad_f * gate_f * sig).astype(jnp.bfloat16)
    hidden = (gate_f * sig * up_f).astype(jnp.bfloat16)
    input_grad = (jnp.dot(gate_grad, w_gate.T, preferred_element_type=jnp.float32)
                  + jnp.dot(up_grad, w_up.T, preferred_element_type=jnp.float32)).astype(jnp.bfloat16)
    down_wgrad = jnp.dot(hidden.T, out_grad, preferred_element_type=jnp.float32).astype(jnp.bfloat16)
    return (input_grad, down_wgrad)
```

```python
import functools

import jax
import jax.numpy as jnp
from jax import lax
from jax.sharding import PartitionSpec as P

CHUNKS = 2


def contract_last(left, right):
    return lax.dot_general(
        left, right, (((1,), (1,)), ((), ())), preferred_element_type=jnp.float32
    )


def contract_first(left, right):
    return lax.dot_general(
        left, right, (((0,), (0,)), ((), ())), preferred_element_type=jnp.float32
    )


def in_order(parts, mine):
    count = len(parts)
    if count == 2:
        first = mine == 0
        return jnp.stack([jnp.where(first, parts[0], parts[1]),
                          jnp.where(first, parts[1], parts[0])])
    turned = jnp.stack([parts[-place % count] for place in range(2 * count)])
    return lax.dynamic_slice_in_dim(turned, (count - mine) % count, count, 0)


def body(cols, lines, gate_pre, up_pre, out_grad, w_gate, w_up, w_down):
    chips = cols // 2
    minors = max(m for m in (1, 2, 4, 8, 16) if m * m <= lines and lines % m == 0)
    majors = lines // minors
    col, row = lax.axis_index("col"), lax.axis_index("row")
    chip, core = col // 2, col % 2
    major, minor = row // minors, row % minors
    units = gate_pre.shape[1]
    tokens, features = out_grad.shape
    step = tokens // CHUNKS
    all_rows = lines * step
    rows = all_rows // cols

    def other_core(block):
        return lax.ppermute(block, "col", [(i, i ^ 1) for i in range(cols)])

    def other_chip(block, hop):
        return lax.ppermute(
            block, "col", [(i, (i // 2 + hop) % chips * 2 + i % 2) for i in range(cols)]
        )

    def along_major(block, hop):
        return lax.ppermute(
            block, "row",
            [(i, (i // minors + hop) % majors * minors + i % minors) for i in range(lines)],
        )

    def along_minor(block, hop):
        return lax.ppermute(
            block, "row",
            [(i, i // minors * minors + (i + hop) % minors) for i in range(lines)],
        )

    def both_cores(mine):
        theirs = other_core(mine)
        first = core == 0
        even = jnp.where(first, mine, theirs)
        odd = jnp.where(first, theirs, mine)
        return jnp.stack([even, odd], axis=1).reshape(all_rows, units)

    majors_grad = [out_grad] + [along_major(out_grad, hop) for hop in range(1, majors)]
    lines_grad = [
        in_order([block] + [along_minor(block, hop) for hop in range(1, minors)], minor)
        for block in majors_grad
    ]
    grads = in_order(lines_grad, major).reshape(lines, CHUNKS, step, features)
    pre = [
        in_order([block] + [other_chip(block, hop) for hop in range(1, chips)], chip)
        .reshape(chips, lines // cols, CHUNKS, step, units)
        for block in (gate_pre, up_pre)
    ]

    inputs, hiddens, grad_chunks = [], [], []
    for i in range(CHUNKS):
        gate_f, up_f = (
            block[:, :, i].reshape(chips, rows, units).astype(jnp.float32) for block in pre
        )
        grad_chunk = grads[:, i].reshape(all_rows, features)
        grad_chunks.append(grad_chunk)
        part = contract_last(grad_chunk, w_down).astype(jnp.bfloat16)
        part = part.reshape(chips, 2, rows, units)
        first = core == 0
        keep = jnp.where(first, part[:, 0], part[:, 1])
        send = jnp.where(first, part[:, 1], part[:, 0])
        pair = (keep.astype(jnp.float32) + other_core(send).astype(jnp.float32)).astype(jnp.bfloat16)
        total = pair.astype(jnp.float32)
        for hop in range(1, chips):
            total = total + other_chip(pair, hop).astype(jnp.float32)
        hidden_grad = total.astype(jnp.bfloat16).astype(jnp.float32)
        sig = jax.nn.sigmoid(gate_f)
        gate_grad = (hidden_grad * up_f * sig * (1.0 + gate_f * (1.0 - sig))).astype(jnp.bfloat16)
        up_grad = (hidden_grad * gate_f * sig).astype(jnp.bfloat16)
        hiddens.append(both_cores((gate_f * sig * up_f).astype(jnp.bfloat16)))
        gate_all, up_all = both_cores(gate_grad), both_cores(up_grad)
        share = contract_last(gate_all, w_gate) + contract_last(up_all, w_up)
        share = share.astype(jnp.bfloat16).reshape(majors, minors, step, features)

        def for_minor(hop):
            at = (minor + hop) % minors
            return lax.dynamic_slice_in_dim(share, at, 1, 1)[:, 0]

        line = for_minor(0).astype(jnp.float32)
        for hop in range(1, minors):
            line = line + along_minor(for_minor(hop), hop).astype(jnp.float32)

        def for_major(hop):
            at = (major + hop) % majors
            return lax.dynamic_slice_in_dim(line, at, 1, 0)[0]

        result = for_major(0)
        for hop in range(1, majors):
            sent = along_major(for_major(hop).astype(jnp.bfloat16), hop)
            result = result + sent.astype(jnp.float32)
        inputs.append(result.astype(jnp.bfloat16))
    down = contract_first(jnp.concatenate(hiddens), jnp.concatenate(grad_chunks))
    return (jnp.concatenate(inputs), down.astype(jnp.bfloat16))


def solution(mesh):
    in_specs = (
        P("col", "row"),
        P("col", "row"),
        P("row", "col"),
        P("col", "row"),
        P("col", "row"),
        P("row", "col"),
    )
    out_specs = (P("row", "col"), P("row", "col"))
    return jax.shard_map(
        functools.partial(body, mesh.shape["col"], mesh.shape["row"]),
        mesh=mesh, in_specs=in_specs, out_specs=out_specs, check_vma=False,
    )
```

```python
import functools

import jax
import jax.numpy as jnp
from jax import lax
from jax.sharding import PartitionSpec as P

CHUNKS = 2


def contract_last(left, right):
    return lax.dot_general(
        left, right, (((1,), (1,)), ((), ())), preferred_element_type=jnp.float32
    )


def contract_first(left, right):
    return lax.dot_general(
        left, right, (((0,), (0,)), ((), ())), preferred_element_type=jnp.float32
    )


def in_order(parts, mine):
    count = len(parts)
    if count == 2:
        first = mine == 0
        return jnp.stack([jnp.where(first, parts[0], parts[1]),
                          jnp.where(first, parts[1], parts[0])])
    turned = jnp.stack([parts[-place % count] for place in range(2 * count)])
    return lax.dynamic_slice_in_dim(turned, (count - mine) % count, count, 0)


def body(cols, lines, gate_pre, up_pre, out_grad, w_gate, w_up, w_down):
    chips = cols // 2
    minors = max(m for m in (1, 2, 4, 8, 16) if m * m <= lines and lines % m == 0)
    majors = lines // minors
    col, row = lax.axis_index("col"), lax.axis_index("row")
    chip, core = col // 2, col % 2
    major, minor = row // minors, row % minors
    units = gate_pre.shape[1]
    tokens, features = out_grad.shape
    step = tokens // CHUNKS
    all_rows = lines * step
    rows = all_rows // cols

    def other_core(block):
        return lax.ppermute(block, "col", [(i, i ^ 1) for i in range(cols)])

    def other_chip(block, hop):
        return lax.ppermute(
            block, "col", [(i, (i // 2 + hop) % chips * 2 + i % 2) for i in range(cols)]
        )

    def along_major(block, hop):
        return lax.ppermute(
            block, "row",
            [(i, (i // minors + hop) % majors * minors + i % minors) for i in range(lines)],
        )

    def along_minor(block, hop):
        return lax.ppermute(
            block, "row",
            [(i, i // minors * minors + (i + hop) % minors) for i in range(lines)],
        )

    def both_cores(mine):
        theirs = other_core(mine)
        first = core == 0
        even = jnp.where(first, mine, theirs)
        odd = jnp.where(first, theirs, mine)
        return jnp.stack([even, odd], axis=1).reshape(all_rows, units)

    def gathered(block):
        lines_grad = []
        for hop in range(majors):
            at = along_major(block, hop) if hop else block
            lines_grad.append(
                in_order([at] + [along_minor(at, m) for m in range(1, minors)], minor)
            )
        return in_order(lines_grad, major).reshape(all_rows, features)

    grad_chunks = [gathered(out_grad[i * step:(i + 1) * step]) for i in range(CHUNKS)]
    pre = [
        in_order([block] + [other_chip(block, hop) for hop in range(1, chips)], chip)
        .reshape(chips, lines // cols, CHUNKS, step, units)
        for block in (gate_pre, up_pre)
    ]

    totals, hiddens = [], []
    first = core == 0
    for i in range(CHUNKS):
        gate_f, up_f = (
            block[:, :, i].reshape(chips, rows, units).astype(jnp.float32) for block in pre
        )
        grad_chunk = grad_chunks[i]
        if totals:
            grad_chunk, part = lax.optimization_barrier((grad_chunk, part))
        part = contract_last(grad_chunk, w_down).astype(jnp.bfloat16)
        halves = part.reshape(chips, 2, rows, units)
        keep = jnp.where(first, halves[:, 0], halves[:, 1])
        send = jnp.where(first, halves[:, 1], halves[:, 0])
        pair = (keep.astype(jnp.float32) + other_core(send).astype(jnp.float32)).astype(jnp.bfloat16)
        total = pair.astype(jnp.float32)
        for hop in range(1, chips):
            total = total + other_chip(pair, hop).astype(jnp.float32)
        totals.append(total)
        sig = jax.nn.sigmoid(gate_f)
        hiddens.append(both_cores((gate_f * sig * up_f).astype(jnp.bfloat16)))
    hidden_all, part = lax.optimization_barrier((jnp.concatenate(hiddens), part))
    down = contract_first(hidden_all, jnp.concatenate(grad_chunks)).astype(jnp.bfloat16)
    last, inputs = down, []
    for i in range(CHUNKS):
        gate_in, up_in, last = lax.optimization_barrier((*pre, last))
        gate_f, up_f = (
            block[:, :, i].reshape(chips, rows, units).astype(jnp.float32)
            for block in (gate_in, up_in)
        )
        sig = jax.nn.sigmoid(gate_f)
        hidden_grad = totals[i].astype(jnp.bfloat16).astype(jnp.float32)
        gate_grad = (hidden_grad * up_f * sig * (1.0 + gate_f * (1.0 - sig))).astype(jnp.bfloat16)
        up_grad = (hidden_grad * gate_f * sig).astype(jnp.bfloat16)
        gate_all, up_all = both_cores(gate_grad), both_cores(up_grad)
        gate_all, up_all, last = lax.optimization_barrier((gate_all, up_all, last))
        if i == 0:
            down = last
        share = contract_last(gate_all, w_gate) + contract_last(up_all, w_up)
        last = share
        share = share.astype(jnp.bfloat16).reshape(majors, minors, step, features)

        def for_minor(hop):
            at = (minor + hop) % minors
            return lax.dynamic_slice_in_dim(share, at, 1, 1)[:, 0]

        line = for_minor(0).astype(jnp.float32)
        for hop in range(1, minors):
            line = line + along_minor(for_minor(hop), hop).astype(jnp.float32)

        def for_major(hop):
            at = (major + hop) % majors
            return lax.dynamic_slice_in_dim(line, at, 1, 0)[0]

        result = for_major(0)
        for hop in range(1, majors):
            sent = along_major(for_major(hop).astype(jnp.bfloat16), hop)
            result = result + sent.astype(jnp.float32)
        inputs.append(result.astype(jnp.bfloat16))
    return (jnp.concatenate(inputs), down)


def solution(mesh):
    in_specs = (
        P("col", "row"),
        P("col", "row"),
        P("row", "col"),
        P("col", "row"),
        P("col", "row"),
        P("row", "col"),
    )
    out_specs = (P("row", "col"), P("row", "col"))
    return jax.shard_map(
        functools.partial(body, mesh.shape["col"], mesh.shape["row"]),
        mesh=mesh, in_specs=in_specs, out_specs=out_specs, check_vma=False,
    )
```
